128 devices in a mesh: row: 8 (over z, x_lo), col: 16 (over x_hi, y, core).
Axes of the slice: x: 4 (x_hi: 2, x_lo: 2; x = x_hi * 2 + x_lo), y: 4, z: 4, core: 2. Of those that a mesh axis runs over, the one named last changes fastest.
Arguments:
- cotangent: float32 [8192, 16384], P('row', 'col'), may hold values from -6 to 6
- whitened: float32 [8192, 16384], P('row', 'col'), may hold values from -0.046875 to 0.046875
- panel_rows: float32 [4, 256, 8192], P(None, None, 'row'), may hold values from -0.375 to 0.375
- diag_inverse: float32 [4, 256, 256], replicated, as said below
Outputs:
- adjoint_rhs: float32 [8192, 16384], P('row', 'col')
- factor_grad: float32 [4, 256, 8192], P(None, 'col', 'row')
The draws below stay inside these ranges and needn't reach their ends.
Inputs may be any that keep to these rules, and one draw needn't show every extreme that they name: `diag_inverse`: each block is lower triangular with diagonal entries between 0.5 and 1.5.
All inputs are finite; a program needn't handle non-finite values.
Results may differ from the reference program's by a relative error of at most 0.00017.
Values sent between devices are 32-bit elements; how exact they have to be, the bound alone decides.
No kernel may reach another device: no remote copies, remote signals or barrier semaphores. Data moves between devices by JAX's collectives and lax.ppermute only.
A program may use at most 128 MiB of HBM per device.

```python
import math
import jax
import jax.numpy as jnp
from jax import lax

NB = 256
PANELS = 4
ROWS_DEV = 1024
M = 8192
RHS = 16384
N_ROW = 8


def draw_diag_inverse(key, part):
    first, second = jax.random.split(jax.random.fold_in(key, 17))
    lower = jax.random.normal(first, (PANELS, NB, NB), jnp.float32) / math.sqrt(NB)
    diagonal = jax.random.uniform(second, (PANELS, NB), jnp.float32, 0.5, 1.5)
    return jnp.tril(lower, -1) + diagonal[:, :, None] * jnp.eye(NB, dtype=jnp.float32)[None]


def steps_of(key, extent, cuts, smallest, largest):
    def one(dim, blocks):
        draws = jax.random.uniform(jax.random.fold_in(jax.random.fold_in(key, 6), dim), (blocks,), jnp.float32, smallest / len(cuts), largest / len(cuts))
        return jnp.repeat(jnp.exp(draws), extent[dim] // blocks).reshape((-1,) + (1,) * (len(extent) - dim - 1))

    level = one(*cuts[0])
    for cut in cuts[1:]:
        level = level * one(*cut)
    return level


def centred(own_key, extent, scale, reach, pieces=(), kind=jnp.bfloat16):
    gain = steps_of(own_key, extent, pieces, -0.22, 0.18) if pieces else 1.0
    result = jax.random.normal(own_key, extent, jnp.float32) * scale * gain
    return jnp.minimum(jnp.maximum(result, -reach), reach).astype(kind)


def setup_inputs(seed: int = 0) -> dict:
    key_of = jax.random.split(jax.random.key(seed), 5)
    cotangent = centred(key_of[0], (M, RHS), 1.0, 6.0, ((0, 8), (1, 16)), jnp.float32)
    whitened = centred(key_of[1], (M, RHS), RHS ** -0.5, 0.046875, ((0, 8), (1, 16)), jnp.float32)
    panel_rows = centred(key_of[2], (PANELS, NB, M), NB ** -0.5, 0.375, ((2, 8),), jnp.float32)
    diag_inverse = draw_diag_inverse(jax.random.fold_in(key_of[4], 71), 0)
    return {"cotangent": cotangent, "whitened": whitened, "panel_rows": panel_rows, "diag_inverse": diag_inverse}


def reference(cotangent, whitened, panel_rows, diag_inverse):
    hi = lax.Precision.HIGHEST
    stored = jnp.arange(M, dtype=jnp.int32)
    natural = ((stored % ROWS_DEV) // NB) * N_ROW + stored // ROWS_DEV
    within = stored % NB
    inner = jnp.arange(NB, dtype=jnp.int32)
    blocks = M // NB
    residual = cotangent
    grads = []
    for p in range(PANELS):
        target = blocks - 1 - p
        start = (N_ROW - 1 - p) * ROWS_DEV + ROWS_DEV - NB
        solved = jnp.dot(diag_inverse[p].T, residual[start:start + NB], precision=hi, preferred_element_type=jnp.float32)
        masked = jnp.where((natural < target)[None, :], panel_rows[p], 0.0)
        update = lax.dot_general(masked, solved, (((0,), (0,)), ((), ())), precision=hi, preferred_element_type=jnp.float32)
        residual = residual - update
        residual = jnp.concatenate([residual[:start], solved, residual[start + NB:]], 0)
        term = lax.dot_general(solved, whitened, (((1,), (1,)), ((), ())), precision=hi, preferred_element_type=jnp.float32)
        keep = (natural[None, :] < target) | ((natural[None, :] == target) & (inner[:, None] >= within[None, :]))
        grads.append(-jnp.where(keep, term, 0.0))
    return residual, jnp.stack(grads)
```

```python
import jax
import jax.numpy as jnp
from jax import lax
from jax.sharding import PartitionSpec as P

HIGH = lax.Precision.HIGH
WIDTH = 256
HALF = 128


def row_pairs(moves, flip=False):
    return [(2 * a + x, 2 * b + ((1 - x) if flip else x)) for a, b in moves for x in range(2)]


def col_pairs(dy=0, flip_core=False, flip_high=False):
    pairs = []
    for xh in range(2):
        for y in range(4):
            for core in range(2):
                src = (xh * 4 + y) * 2 + core
                dst = ((xh ^ flip_high) * 4 + (y + dy) % 4) * 2 + (core ^ flip_core)
                pairs.append((src, dst))
    return pairs


def send_row(v, moves, flip=False):
    return lax.ppermute(v, "row", row_pairs(moves, flip))


def send_col(v, **kw):
    return lax.ppermute(v, "col", col_pairs(**kw))


def together(*arrays):
    return lax.optimization_barrier(arrays)


def take(a, i, axis):
    return lax.dynamic_index_in_dim(a, i, axis, keepdims=False)


def dot(a, b, ca, cb):
    return lax.dot_general(a, b, (((ca,), (cb,)), ((), ())), precision=HIGH, preferred_element_type=jnp.float32)


def gather_blocks(block, z, x):
    source = z >= 2
    zero_or_three = (z == 0) | (z == 3)
    b1, b2 = block[:HALF], block[HALF:]
    up, down = [(3, 0), (2, 3)], [(3, 2), (2, 1)]
    zp1, zm1, x1 = send_row(b1, up), send_row(b1, down), send_row(b1, [(2, 2), (3, 3)], True)
    zp1, zm1, x1 = together(zp1, zm1, x1)
    a1 = jnp.where(zero_or_three, zp1, zm1)
    every = [(i, i) for i in range(4)]
    out2 = together(jnp.where(source, b2, a1))[0]
    up2, down2 = up + [(0, 1)], down + [(1, 0)]
    zp2, zm2, x2 = send_row(out2, up2), send_row(out2, down2), send_row(out2, every, True)
    zp2, zm2, x2 = together(zp2, zm2, x2)
    a2 = jnp.where(zero_or_three, zp2, zm2)
    fwd2 = jnp.where(zero_or_three, zm2, zp2)
    o3p = jnp.where(z == 3, x2, jnp.where(z == 2, x1, zp2))
    o3m = jnp.where(z == 2, x2, jnp.where(z == 3, x1, zm2))
    o3x = jnp.where(source, a2, fwd2)
    o3p, o3m, o3x = together(o3p, o3m, o3x)
    zp3, zm3, x3 = send_row(o3p, up2), send_row(o3m, down2), send_row(o3x, every, True)
    zp3, zm3, x3 = together(zp3, zm3, x3)
    a3 = jnp.where(zero_or_three, zp3, zm3)
    fwd3 = jnp.where(zero_or_three, zm3, zp3)
    o4x, o4n = together(fwd3[: HALF // 2], a3[HALF // 2 :])
    x4 = send_row(o4x, [(0, 0), (1, 1)], True)
    n4 = send_row(o4n, [(0, 1), (1, 0)])
    x4, n4 = together(x4, n4)
    last = jnp.concatenate([x4, n4], 0)
    k_x = [jnp.where(source, b1, a1), jnp.where(source, b2, a2)]
    k_o = [jnp.where(source, x1, x2), jnp.where(source, x2, a3)]
    l_x = [jnp.where(source, a1, fwd2), jnp.where(source, a2, fwd3)]
    l_o = [jnp.where(source, a3, x3), jnp.where(source, x3, last)]

    def pick(c, a, b):
        return [jnp.where(c, s, t) for s, t in zip(a, b)]

    k1, k0 = pick(x == 1, k_x, k_o), pick(x == 1, k_o, k_x)
    l1, l0 = pick(x == 1, l_x, l_o), pick(x == 1, l_o, l_x)
    blocks = [
        pick(zero_or_three, k1, l1),
        pick(zero_or_three, k0, l0),
        pick(zero_or_three, l1, k1),
        pick(zero_or_three, l0, k0),
    ]
    return [jnp.concatenate(b, 0) for b in blocks]


COUPLED = [(0, 1), (0, 2), (1, 2), (0, 3), (1, 3), (2, 3)]


def gather_couplings(last, device, z, y, core):
    part = 32
    eighth = y * 2 + core
    mine = lax.dynamic_slice_in_dim(last, eighth * part, part, 1)
    table = jnp.stack([jnp.where(device == 7 - p, mine[q], 0.0) for q, p in COUPLED])
    table = table + send_row(table, [(2, 2), (3, 3)], True)
    table = table + send_row(table, [(2, 3), (3, 2)])
    table = jnp.where(z >= 2, table, send_row(table, [(3, 0), (2, 1)]))
    sent = [table] + [send_col(table, dy=d) for d in (1, 2, 3)]
    rows = [jnp.stack(sent)]
    rel = rows[0]
    ordered = jnp.stack([take(rel, lax.rem(y - t + 4, 4), 0) for t in range(4)])
    other = send_col(ordered, flip_core=True)
    first = jnp.where(core == 0, ordered, other)
    second = jnp.where(core == 0, other, ordered)
    full = jnp.stack([first, second], 1)
    return full.transpose(2, 0, 1, 3, 4).reshape(6, WIDTH, WIDTH)


def reduce_scatter(g, xh, y, core):
    n, _, c = g.shape
    g = g.reshape(n, 2, 4, 2, 16, c)
    h = take(g, core, 3) + send_col(take(g, 1 - core, 3), flip_core=True)
    parts = [send_col(take(h, lax.rem(y + d, 4), 2), dy=d) for d in (1, 3, 2)]
    k = take(h, y, 2) + parts[0] + parts[1] + parts[2]
    return take(k, xh, 1) + send_col(take(k, 1 - xh, 1), flip_high=True)


def body(cotangent, whitened, panel_rows, diag_inverse):
    device = lax.axis_index("row")
    column = lax.axis_index("col")
    z, x = device // 2, device % 2
    xh, y, core = column // 8, (column // 2) % 4, column % 2
    rows = cotangent.shape[0]
    top = rows - WIDTH
    panels = panel_rows.shape[0]
    owned = 7 - device

    couplings = gather_couplings(panel_rows[:, :, top:], device, z, y, core)
    raw = gather_blocks(cotangent[top:], z, x)

    solved = []
    for p in range(panels):
        r = raw[p]
        for q in range(p):
            r = r - dot(couplings[COUPLED.index((q, p))], solved[q], 0, 0)
        solved.append(dot(diag_inverse[p], r, 0, 0))
    grads = []
    for group in ((0, 1), (2, 3)):
        stacked = jnp.concatenate([solved[p] for p in group], 0)
        term = dot(stacked, whitened, 1, 1).reshape(len(group), WIDTH, rows)
        grads.append(reduce_scatter(term, xh, y, core))
    grad = jnp.concatenate(grads, 0)
    local = jnp.arange(rows, dtype=jnp.int32)
    natural = local // WIDTH * 8 + device
    within = local % WIDTH
    inner = column * 16 + jnp.arange(16, dtype=jnp.int32)
    target = 31 - jnp.arange(panels, dtype=jnp.int32)
    keep = (natural[None, None, :] < target[:, None, None]) | (
        (natural[None, None, :] == target[:, None, None]) & (inner[None, :, None] >= within[None, None, :])
    )
    grad = jnp.where(keep, -grad, 0.0)

    every = jnp.concatenate(solved, 0)
    masked = jnp.where((natural[None, :] < target[:, None])[:, None, :], panel_rows, 0.0)
    residual = cotangent - dot(masked.reshape(panels * WIDTH, rows), every, 0, 0)
    own = lax.dynamic_slice_in_dim(every, jnp.clip(owned, 0, 3) * WIDTH, WIDTH, 0)
    tail = jnp.where(device >= 4, own, residual[top:])
    residual = lax.dynamic_update_slice_in_dim(residual, tail, top, 0)
    return residual, grad


def solution(mesh):
    return jax.shard_map(
        body,
        mesh=mesh,
        in_specs=(P("row", "col"), P("row", "col"), P(None, None, "row"), P()),
        out_specs=(P("row", "col"), P(None, "col", "row")),
        check_vma=False,
    )
```

```python
import jax
import jax.numpy as jnp
from jax import lax
from jax.experimental import pallas as pl
from jax.experimental.pallas import tpu as pltpu
from jax.sharding import PartitionSpec as P

HIGH = lax.Precision.HIGH
WIDTH = 256


Z_GROUPS = [[2 * z + x for z in range(4)] for x in range(2)]
X_SWAP = [(r, r ^ 1) for r in range(8)]
HALVES = [(7, 3), (6, 2), (5, 1), (4, 0)]
Y_GROUPS = [[(xh * 4 + y) * 2 + core for y in range(4)] for xh in range(2) for core in range(2)]
CORE_SWAP = [(c, c ^ 1) for c in range(16)]
Y_STEPS = [[(c, c // 8 * 8 + (c + 2 * d) % 8) for c in range(16)] for d in (1, 3, 2)]
HIGH_SWAP = [(c, c ^ 8) for c in range(16)]


def exchange(pieces, axis, groups=None):
    return lax.all_to_all(pieces, axis, 0, 0, axis_index_groups=groups)


def copies(a, n):
    return jnp.broadcast_to(a[None], (n,) + a.shape)


def together(*arrays):
    return lax.optimization_barrier(arrays)


def take(a, i, axis):
    return lax.dynamic_index_in_dim(a, i, axis, keepdims=False)


def dot(a, b, ca, cb):
    return lax.dot_general(a, b, (((ca,), (cb,)), ((), ())), precision=HIGH, preferred_element_type=jnp.float32)


COUPLED = [(0, 1), (0, 2), (1, 2), (0, 3), (1, 3), (2, 3)]
PART = WIDTH // 8


def couplings_over_row(last, y, core):
    mine = lax.dynamic_slice_in_dim(last, (y * 2 + core) * PART, PART, 1)
    with jax.named_scope("coupling_row"):
        got = exchange(copies(mine.reshape(3 * PART, WIDTH), 8), "row").reshape(8, 3, PART, WIDTH)
    return jnp.concatenate([got[7 - p, q] for q, p in COUPLED], 0)


def couplings_over_y(table):
    with jax.named_scope("coupling_y"):
        return jnp.stack([table] + [lax.ppermute(table, "col", pairs) for pairs in Y_STEPS])


def split(a):
    high = a.astype(jnp.bfloat16)
    return high, (a - high.astype(jnp.float32)).astype(jnp.bfloat16)


def product(a, b):
    def one(s, t):
        return jnp.dot(s, t, preferred_element_type=jnp.float32)

    return one(a[0], b[0]) + (one(a[0], b[1]) + one(a[1], b[0]))


def solve_kernel(
    place, over_z, peer, both, same, swapped, diagonal, out, ordered, raw, coupling, left_high, left_low, high, low
):
    x, y_index, core = place[0], place[1], place[2]

    @pl.when(pl.program_id(0) == 0)
    def _():
        for r, back in enumerate((0, 1, 3, 2)):
            from_y = lax.rem(y_index + (4 - back), 4)
            for part, c in ((same, core), (swapped, 1 - core)):
                start = pl.multiple_of((from_y * 2 + c) * PART, PART)
                for i in range(6):
                    coupling[i, pl.ds(start, PART)] = part[r, PART * i : PART * (i + 1)]
        for i, (q, p) in enumerate(COUPLED):
            at = slice(WIDTH * q, WIDTH * (q + 1))
            left_high[p, :, at], left_low[p, :, at] = split(coupling[i].T)
        for p in range(4):
            at = slice(WIDTH * p, WIDTH * (p + 1))
            left_high[p, :, at], left_low[p, :, at] = split(diagonal[p])

    for pair, z in ((0, 3), (1, 2)):
        mine = [over_z[z], both[z, 0], over_z[z - 2], both[z - 2, 0]]
        other = [peer[z], both[z, 1], peer[z - 2], both[z - 2, 1]]
        for i in range(4):
            for panel, part in ((1 - x, mine[i]), (x, other[i])):
                raw[pl.ds(pl.multiple_of((2 * pair + panel) * WIDTH + 64 * i, 64), 64)] = part
    for p in range(4):
        done, at = slice(0, WIDTH * p), slice(WIDTH * p, WIDTH * (p + 1))
        acc = raw[at]
        if p:
            acc = acc - product((left_high[p, :, done], left_low[p, :, done]), (high[done], low[done]))
        y = product((left_high[p, :, at], left_low[p, :, at]), split(acc))
        out[at] = y
        for xh in range(2):
            for yy in range(4):
                for c in range(2):
                    inside = yy * 64 + xh * 32 if p < 2 else xh * 128 + yy * 32
                    to, of = p // 2 * 512 + c * 256 + inside + p % 2 * 16, 16 * ((xh * 4 + yy) * 2 + c)
                    ordered[to : to + 16] = y[of : of + 16]
        if p < 3:
            high[at], low[at] = split(y)


def solve(place, over_z, peer, both, same, swapped, diagonal):
    rows = over_z.shape[-1]
    tile = 512
    whole = pl.BlockSpec((4, 6 * PART, WIDTH), lambda j: (0, 0, 0))
    result = jax.ShapeDtypeStruct((4 * WIDTH, rows), jnp.float32)
    return pl.pallas_call(
        solve_kernel,
        out_shape=[result, result],
        grid=(rows // tile,),
        in_specs=[
            pl.BlockSpec(memory_space=pltpu.SMEM),
            pl.BlockSpec((4, 64, tile), lambda j: (0, 0, j)),
            pl.BlockSpec((4, 64, tile), lambda j: (0, 0, j)),
            pl.BlockSpec((4, 2, 64, tile), lambda j: (0, 0, 0, j)),
            whole,
            whole,
            pl.BlockSpec((4, WIDTH, WIDTH), lambda j: (0, 0, 0)),
        ],
        out_specs=[pl.BlockSpec((4 * WIDTH, tile), lambda j: (0, j))] * 2,
        scratch_shapes=[
            pltpu.VMEM((4 * WIDTH, tile), jnp.float32),
            pltpu.VMEM((6, WIDTH, WIDTH), jnp.float32),
            pltpu.VMEM((4, WIDTH, 4 * WIDTH), jnp.bfloat16),
            pltpu.VMEM((4, WIDTH, 4 * WIDTH), jnp.bfloat16),
            pltpu.VMEM((3 * WIDTH, tile), jnp.bfloat16),
            pltpu.VMEM((3 * WIDTH, tile), jnp.bfloat16),
        ],
        compiler_params=pltpu.CompilerParams(vmem_limit_bytes=40 * 1024 * 1024),
        cost_estimate=pl.CostEstimate(flops=6 * 10 * WIDTH * WIDTH * rows, bytes_accessed=15 * 2**20, transcendentals=0),
    )(place, over_z, peer, both, same, swapped, diagonal)


def solve_panels(block, last, device, y, core, early):
    half = block.shape[0] // 2
    table = couplings_over_row(last, y, core)
    with jax.named_scope("halves"):
        sent = lax.ppermute(block[half:], "row", HALVES)
    shard = jnp.where(device >= 4, block[:half], sent)
    a, b = shard[: half // 2], shard[half // 2 :]
    with jax.named_scope("first"):
        a, b, table, *early = together(a, b, table, *early)
        over_z = exchange(copies(a, 4), "row", Z_GROUPS)
        over_x = lax.ppermute(b, "row", X_SWAP)
        over_z, second, same = together(over_z, jnp.concatenate([b, over_x], 0), couplings_over_y(table))
    with jax.named_scope("second"):
        both = exchange(copies(second, 4), "row", Z_GROUPS)
        peer = lax.ppermute(over_z, "row", X_SWAP)
        swapped = lax.ppermute(same, "col", CORE_SWAP)
    both = both.reshape(4, 2, half // 2, -1)
    place = jnp.stack([device % 2, y, core])
    return solve(place, over_z, peer, both, same, swapped, early[0]), early[1:]


def part_and_rest(a, index, axis_pairs):
    a = a.reshape(2, -1, a.shape[-1])
    return take(a, index, 0) + lax.ppermute(take(a, 1 - index, 0), "col", axis_pairs)


def over_y(a):
    return exchange(a.reshape(4, -1, a.shape[-1]), "col", Y_GROUPS).sum(0)


def body(cotangent, whitened, panel_rows, diag_inverse):
    device = lax.axis_index("row")
    column = lax.axis_index("col")
    xh, y, core = column // 8, (column // 2) % 4, column % 2
    rows = cotangent.shape[0]
    top = rows - WIDTH
    panels = panel_rows.shape[0]
    owned = 7 - device

    local = jnp.arange(rows, dtype=jnp.int32)
    natural = local // WIDTH * 8 + device
    within = local % WIDTH
    inner = column * 16 + jnp.arange(16, dtype=jnp.int32)
    target = 31 - jnp.arange(panels, dtype=jnp.int32)
    masked = jnp.where((natural[None, :] < target[:, None])[:, None, :], panel_rows, 0.0)
    masked = masked.reshape(panels * WIDTH, rows)

    (every, ordered), (masked,) = solve_panels(
        cotangent[top:], panel_rows[: panels - 1, :, top:], device, y, core, [diag_inverse.transpose(0, 2, 1), masked]
    )

    half = 2 * WIDTH
    h_first = part_and_rest(dot(ordered[:half], whitened, 1, 1), core, CORE_SWAP)
    h_second = part_and_rest(dot(ordered[half:], whitened, 1, 1), core, CORE_SWAP)
    every = together(every, h_first, h_second)[0]
    residual = cotangent - dot(masked, every, 0, 0)
    k_first, k_second = over_y(h_first), part_and_rest(h_second, xh, HIGH_SWAP)
    residual, k_first, k_second = together(residual, k_first, k_second)
    grad = jnp.concatenate([part_and_rest(k_first, xh, HIGH_SWAP), over_y(k_second)], 0)
    grad = grad.reshape(panels, 16, rows)
    keep = (natural[None, None, :] < target[:, None, None]) | (
        (natural[None, None, :] == target[:, None, None]) & (inner[None, :, None] >= within[None, None, :])
    )
    grad = jnp.where(keep, -grad, 0.0)

    own = lax.dynamic_slice_in_dim(every, jnp.clip(owned, 0, 3) * WIDTH, WIDTH, 0)
    tail = jnp.where(device >= 4, own, residual[top:])
    residual = lax.dynamic_update_slice_in_dim(residual, tail, top, 0)
    return residual, grad


def solution(mesh):
    return jax.shard_map(
        body,
        mesh=mesh,
        in_specs=(P("row", "col"), P("row", "col"), P(None, None, "row"), P()),
        out_specs=(P("row", "col"), P(None, "col", "row")),
        check_vma=False,
    )
```

```python
import jax
import jax.numpy as jnp
from jax import lax
from jax.experimental import pallas as pl
from jax.experimental.pallas import tpu as pltpu
from jax.sharding import PartitionSpec as P

HIGH = lax.Precision.HIGH
WIDTH = 256


Z_GROUPS = [[2 * z + x for z in range(4)] for x in range(2)]
X_SWAP = [(r, r ^ 1) for r in range(8)]
HALVES = [(7, 3), (6, 2), (5, 1), (4, 0)]
Y_GROUPS = [[(xh * 4 + y) * 2 + core for y in range(4)] for xh in range(2) for core in range(2)]
CORE_SWAP = [(c, c ^ 1) for c in range(16)]
Y_STEPS = [[(c, c // 8 * 8 + (c + 2 * d) % 8) for c in range(16)] for d in (1, 3, 2)]
CORE_GROUPS = [[2 * i + core for i in range(8)] for core in range(2)]


def exchange(pieces, axis, groups=None):
    return lax.all_to_all(pieces, axis, 0, 0, axis_index_groups=groups)


def copies(a, n):
    return jnp.broadcast_to(a[None], (n,) + a.shape)


def together(*arrays):
    return lax.optimization_barrier(arrays)


def take(a, i, axis):
    return lax.dynamic_index_in_dim(a, i, axis, keepdims=False)


def dot(a, b, ca, cb):
    return lax.dot_general(a, b, (((ca,), (cb,)), ((), ())), precision=HIGH, preferred_element_type=jnp.float32)


COUPLED = [(0, 1), (0, 2), (1, 2), (0, 3), (1, 3), (2, 3)]
PART = WIDTH // 8


def couplings_over_row(last, y, core):
    mine = lax.dynamic_slice_in_dim(last, (y * 2 + core) * PART, PART, 1)
    with jax.named_scope("coupling_row"):
        got = exchange(copies(mine.reshape(3 * PART, WIDTH), 8), "row").reshape(8, 3, PART, WIDTH)
    return jnp.concatenate([got[7 - p, q] for q, p in COUPLED], 0)


def couplings_over_y(table):
    with jax.named_scope("coupling_y"):
        return jnp.stack([table] + [lax.ppermute(table, "col", pairs) for pairs in Y_STEPS])


def split(a):
    high = a.astype(jnp.bfloat16)
    return high, (a - high.astype(jnp.float32)).astype(jnp.bfloat16)


def product(a, b):
    def one(s, t):
        return jnp.dot(s, t, preferred_element_type=jnp.float32)

    return one(a[0], b[0]) + (one(a[0], b[1]) + one(a[1], b[0]))


def solve_kernel(
    place, over_z, peer, both, same, swapped, diagonal, ordered, raw, coupling, left_high, left_low, high, low
):
    x, y_index, core = place[0], place[1], place[2]

    @pl.when(pl.program_id(0) == 0)
    def _():
        for r, back in enumerate((0, 1, 3, 2)):
            from_y = lax.rem(y_index + (4 - back), 4)
            for part, c in ((same, core), (swapped, 1 - core)):
                start = pl.multiple_of((from_y * 2 + c) * PART, PART)
                for i in range(6):
                    coupling[i, pl.ds(start, PART)] = part[r, PART * i : PART * (i + 1)]
        for i, (q, p) in enumerate(COUPLED):
            at = slice(WIDTH * q, WIDTH * (q + 1))
            left_high[p, :, at], left_low[p, :, at] = split(coupling[i].T)
        for p in range(4):
            at = slice(WIDTH * p, WIDTH * (p + 1))
            left_high[p, :, at], left_low[p, :, at] = split(diagonal[p])

    for pair, z in ((0, 3), (1, 2)):
        mine = [over_z[z], both[z, 0], over_z[z - 2], both[z - 2, 0]]
        other = [peer[z], both[z, 1], peer[z - 2], both[z - 2, 1]]
        for i in range(4):
            for panel, part in ((1 - x, mine[i]), (x, other[i])):
                raw[pl.ds(pl.multiple_of((2 * pair + panel) * WIDTH + 64 * i, 64), 64)] = part
    for p in range(4):
        done, at = slice(0, WIDTH * p), slice(WIDTH * p, WIDTH * (p + 1))
        acc = raw[at]
        if p:
            acc = acc - product((left_high[p, :, done], left_low[p, :, done]), (high[done], low[done]))
        y = product((left_high[p, :, at], left_low[p, :, at]), split(acc))
        for i in range(8):
            for c in range(2):
                to, of = p // 2 * 512 + c * 256 + i * 32 + p % 2 * 16, 16 * (i * 2 + c)
                ordered[to : to + 16] = y[of : of + 16]
        if p < 3:
            high[at], low[at] = split(y)


def solve(place, over_z, peer, both, same, swapped, diagonal):
    rows = over_z.shape[-1]
    tile = 512
    whole = pl.BlockSpec((4, 6 * PART, WIDTH), lambda j: (0, 0, 0), pipeline_mode=pl.Buffered(1))
    return pl.pallas_call(
        solve_kernel,
        out_shape=jax.ShapeDtypeStruct((4 * WIDTH, rows), jnp.float32),
        grid=(rows // tile,),
        in_specs=[
            pl.BlockSpec(memory_space=pltpu.SMEM),
            pl.BlockSpec((4, 64, tile), lambda j: (0, 0, j)),
            pl.BlockSpec((4, 64, tile), lambda j: (0, 0, j)),
            pl.BlockSpec((4, 2, 64, tile), lambda j: (0, 0, 0, j)),
            whole,
            whole,
            pl.BlockSpec((4, WIDTH, WIDTH), lambda j: (0, 0, 0), pipeline_mode=pl.Buffered(1)),
        ],
        out_specs=pl.BlockSpec((4 * WIDTH, tile), lambda j: (0, j)),
        scratch_shapes=[
            pltpu.VMEM((4 * WIDTH, tile), jnp.float32),
            pltpu.VMEM((6, WIDTH, WIDTH), jnp.float32),
            pltpu.VMEM((4, WIDTH, 4 * WIDTH), jnp.bfloat16),
            pltpu.VMEM((4, WIDTH, 4 * WIDTH), jnp.bfloat16),
            pltpu.VMEM((3 * WIDTH, tile), jnp.bfloat16),
            pltpu.VMEM((3 * WIDTH, tile), jnp.bfloat16),
        ],
        compiler_params=pltpu.CompilerParams(vmem_limit_bytes=24 * 1024 * 1024),
        cost_estimate=pl.CostEstimate(flops=6 * 10 * WIDTH * WIDTH * rows, bytes_accessed=11 * 2**20, transcendentals=0),
    )(place, over_z, peer, both, same, swapped, diagonal)


def solve_panels(block, last, device, y, core, early):
    half = block.shape[0] // 2
    table = couplings_over_row(last, y, core)
    with jax.named_scope("halves"):
        sent = lax.ppermute(block[half:], "row", HALVES)
    shard = jnp.where(device >= 4, block[:half], sent)
    a, b = shard[: half // 2], shard[half // 2 :]
    with jax.named_scope("first"):
        a, b, table, *early = together(a, b, table, *early)
        over_z = exchange(copies(a, 4), "row", Z_GROUPS)
        over_x = lax.ppermute(b, "row", X_SWAP)
        over_z, second, same = together(over_z, jnp.concatenate([b, over_x], 0), couplings_over_y(table))
    with jax.named_scope("second"):
        both = exchange(copies(second, 4), "row", Z_GROUPS)
        peer = lax.ppermute(over_z, "row", X_SWAP)
        swapped = lax.ppermute(same, "col", CORE_SWAP)
    both = both.reshape(4, 2, half // 2, -1)
    place = jnp.stack([device % 2, y, core])
    return solve(place, over_z, peer, both, same, swapped, early[0]), early[1:]


def part_and_rest(a, index, axis_pairs):
    a = a.reshape(2, -1, a.shape[-1])
    return take(a, index, 0) + lax.ppermute(take(a, 1 - index, 0), "col", axis_pairs)


def over_eight(a):
    return exchange(a.reshape(8, -1, a.shape[-1]), "col", CORE_GROUPS).sum(0)


def reorder(a):
    c = a.shape[-1]
    return a.reshape(2, 2, 8, 2, 16, c).transpose(0, 3, 2, 1, 4, 5).reshape(-1, c)


def panel_of(ordered, p):
    c = ordered.shape[-1]
    rows = take(take(ordered.reshape(2, 2, 8, 2, 16, c), p // 2, 0), p % 2, 2)
    return rows.transpose(1, 0, 2, 3).reshape(-1, c)


def body(cotangent, whitened, panel_rows, diag_inverse):
    device = lax.axis_index("row")
    column = lax.axis_index("col")
    xh, y, core = column // 8, (column // 2) % 4, column % 2
    rows = cotangent.shape[0]
    top = rows - WIDTH
    panels = panel_rows.shape[0]
    owned = 7 - device

    local = jnp.arange(rows, dtype=jnp.int32)
    natural = local // WIDTH * 8 + device
    within = local % WIDTH
    inner = column * 16 + jnp.arange(16, dtype=jnp.int32)
    target = 31 - jnp.arange(panels, dtype=jnp.int32)
    masked = jnp.where((natural[None, :] < target[:, None])[:, None, :], panel_rows, 0.0)
    masked = reorder(masked)

    ordered, (masked,) = solve_panels(
        cotangent[top:], panel_rows[: panels - 1, :, top:], device, y, core, [diag_inverse.transpose(0, 2, 1), masked]
    )

    half = 2 * WIDTH
    h_first = part_and_rest(dot(ordered[:half], whitened, 1, 1), core, CORE_SWAP)
    h_second = part_and_rest(dot(ordered[half:], whitened, 1, 1), core, CORE_SWAP)
    solved = together(ordered, h_first, h_second)[0]
    residual = cotangent - dot(masked, solved, 0, 0)
    both = jnp.concatenate([h.reshape(8, -1, rows) for h in (h_first, h_second)], 1)
    grad = over_eight(both.reshape(-1, rows))
    grad = grad.reshape(panels, 16, rows)
    keep = (natural[None, None, :] < target[:, None, None]) | (
        (natural[None, None, :] == target[:, None, None]) & (inner[None, :, None] >= within[None, None, :])
    )
    grad = jnp.where(keep, -grad, 0.0)

    own = panel_of(solved, jnp.clip(owned, 0, 3))
    tail = jnp.where(device >= 4, own, residual[top:])
    residual = lax.dynamic_update_slice_in_dim(residual, tail, top, 0)
    return residual, grad


def solution(mesh):
    return jax.shard_map(
        body,
        mesh=mesh,
        in_specs=(P("row", "col"), P("row", "col"), P(None, None, "row"), P()),
        out_specs=(P("row", "col"), P(None, "col", "row")),
        check_vma=False,
    )
```

```python
import jax
import jax.numpy as jnp
from jax import lax
from jax.experimental import pallas as pl
from jax.experimental.pallas import tpu as pltpu
from jax.sharding import PartitionSpec as P

HIGH = lax.Precision.HIGH
WIDTH = 256


Z_GROUPS = [[2 * z + x for z in range(4)] for x in range(2)]
X_SWAP = [(r, r ^ 1) for r in range(8)]
HALVES = [(7, 3), (6, 2), (5, 1), (4, 0)]
Y_GROUPS = [[(xh * 4 + y) * 2 + core for y in range(4)] for xh in range(2) for core in range(2)]
CORE_SWAP = [(c, c ^ 1) for c in range(16)]
Y_STEPS = [[(c, c // 8 * 8 + (c + 2 * d) % 8) for c in range(16)] for d in (1, 3, 2)]
CORE_GROUPS = [[2 * i + core for i in range(8)] for core in range(2)]


def exchange(pieces, axis, groups=None):
    return lax.all_to_all(pieces, axis, 0, 0, axis_index_groups=groups)


def copies(a, n):
    return jnp.broadcast_to(a[None], (n,) + a.shape)


def together(*arrays):
    return lax.optimization_barrier(arrays)


def take(a, i, axis):
    return lax.dynamic_index_in_dim(a, i, axis, keepdims=False)


def dot(a, b, ca, cb):
    return lax.dot_general(a, b, (((ca,), (cb,)), ((), ())), precision=HIGH, preferred_element_type=jnp.float32)


COUPLED = [(0, 1), (0, 2), (1, 2), (0, 3), (1, 3), (2, 3)]
PART = WIDTH // 8


def couplings_over_row(last, y, core):
    mine = lax.dynamic_slice_in_dim(last, (y * 2 + core) * PART, PART, 1)
    with jax.named_scope("coupling_row"):
        got = exchange(copies(mine.reshape(3 * PART, WIDTH), 8), "row").reshape(8, 3, PART, WIDTH)
    return jnp.concatenate([got[7 - p, q] for q, p in COUPLED], 0)


def couplings_over_y(table):
    with jax.named_scope("coupling_y"):
        return jnp.stack([table] + [lax.ppermute(table, "col", pairs) for pairs in Y_STEPS])


def split(a):
    high = a.astype(jnp.bfloat16)
    return high, (a - high.astype(jnp.float32)).astype(jnp.bfloat16)


def product(a, b):
    def one(s, t):
        return jnp.dot(s, t, preferred_element_type=jnp.float32)

    return one(a[0], b[0]) + (one(a[0], b[1]) + one(a[1], b[0]))


def solve_kernel(
    place, over_z, peer, both, same, swapped, diagonal, ordered, raw, coupling, left_high, left_low, high, low
):
    x, y_index, core = place[0], place[1], place[2]

    @pl.when(pl.program_id(0) == 0)
    def _():
        for r, back in enumerate((0, 1, 3, 2)):
            from_y = lax.rem(y_index + (4 - back), 4)
            for part, c in ((same, core), (swapped, 1 - core)):
                start = pl.multiple_of((from_y * 2 + c) * PART, PART)
                for i in range(6):
                    coupling[i, pl.ds(start, PART)] = part[r, PART * i : PART * (i + 1)]
        for i, (q, p) in enumerate(COUPLED):
            at = slice(WIDTH * q, WIDTH * (q + 1))
            left_high[p, :, at], left_low[p, :, at] = split(coupling[i].T)
        for p in range(4):
            at = slice(WIDTH * p, WIDTH * (p + 1))
            left_high[p, :, at], left_low[p, :, at] = split(diagonal[p])

    for pair, z in ((0, 3), (1, 2)):
        mine = [over_z[z], both[z, 0], over_z[z - 2], both[z - 2, 0]]
        other = [peer[z], both[z, 1], peer[z - 2], both[z - 2, 1]]
        for i in range(4):
            for panel, part in ((1 - x, mine[i]), (x, other[i])):
                raw[pl.ds(pl.multiple_of((2 * pair + panel) * WIDTH + 64 * i, 64), 64)] = part
    for p in range(4):
        done, at = slice(0, WIDTH * p), slice(WIDTH * p, WIDTH * (p + 1))
        acc = raw[at]
        if p:
            acc = acc - product((left_high[p, :, done], left_low[p, :, done]), (high[done], low[done]))
        y = product((left_high[p, :, at], left_low[p, :, at]), split(acc))
        for i in range(8):
            for c in range(2):
                to, of = lax.bitwise_xor(core, c) * 512 + i * 64 + p * 16, 16 * (i * 2 + c)
                ordered[pl.ds(pl.multiple_of(to, 16), 16)] = y[of : of + 16]
        if p < 3:
            high[at], low[at] = split(y)


def solve(place, over_z, peer, both, same, swapped, diagonal):
    rows = over_z.shape[-1]
    tile = 512
    whole = pl.BlockSpec((4, 6 * PART, WIDTH), lambda j: (0, 0, 0), pipeline_mode=pl.Buffered(1))
    return pl.pallas_call(
        solve_kernel,
        out_shape=jax.ShapeDtypeStruct((4 * WIDTH, rows), jnp.float32),
        grid=(rows // tile,),
        in_specs=[
            pl.BlockSpec(memory_space=pltpu.SMEM),
            pl.BlockSpec((4, 64, tile), lambda j: (0, 0, j)),
            pl.BlockSpec((4, 64, tile), lambda j: (0, 0, j)),
            pl.BlockSpec((4, 2, 64, tile), lambda j: (0, 0, 0, j)),
            whole,
            whole,
            pl.BlockSpec((4, WIDTH, WIDTH), lambda j: (0, 0, 0), pipeline_mode=pl.Buffered(1)),
        ],
        out_specs=pl.BlockSpec((4 * WIDTH, tile), lambda j: (0, j)),
        scratch_shapes=[
            pltpu.VMEM((4 * WIDTH, tile), jnp.float32),
            pltpu.VMEM((6, WIDTH, WIDTH), jnp.float32),
            pltpu.VMEM((4, WIDTH, 4 * WIDTH), jnp.bfloat16),
            pltpu.VMEM((4, WIDTH, 4 * WIDTH), jnp.bfloat16),
            pltpu.VMEM((3 * WIDTH, tile), jnp.bfloat16),
            pltpu.VMEM((3 * WIDTH, tile), jnp.bfloat16),
        ],
        compiler_params=pltpu.CompilerParams(vmem_limit_bytes=24 * 1024 * 1024),
        cost_estimate=pl.CostEstimate(flops=6 * 10 * WIDTH * WIDTH * rows, bytes_accessed=11 * 2**20, transcendentals=0),
    )(place, over_z, peer, both, same, swapped, diagonal)


def solve_panels(block, last, device, y, core, early):
    half = block.shape[0] // 2
    table = couplings_over_row(last, y, core)
    with jax.named_scope("halves"):
        sent = lax.ppermute(block[half:], "row", HALVES)
    shard = jnp.where(device >= 4, block[:half], sent)
    a, b = shard[: half // 2], shard[half // 2 :]
    with jax.named_scope("first"):
        a, b, table, *early = together(a, b, table, *early)
        over_z = exchange(copies(a, 4), "row", Z_GROUPS)
        over_x = lax.ppermute(b, "row", X_SWAP)
        over_z, second, same = together(over_z, jnp.concatenate([b, over_x], 0), couplings_over_y(table))
    with jax.named_scope("second"):
        both = exchange(copies(second, 4), "row", Z_GROUPS)
        peer = lax.ppermute(over_z, "row", X_SWAP)
        swapped = lax.ppermute(same, "col", CORE_SWAP)
    both = both.reshape(4, 2, half // 2, -1)
    place = jnp.stack([device % 2, y, core])
    return solve(place, over_z, peer, both, same, swapped, early[0]), early[1:]


def over_eight(a):
    return exchange(a.reshape(8, -1, a.shape[-1]), "col", CORE_GROUPS).sum(0)


def reorder(a, core):
    c = a.shape[-1]
    a = a.reshape(4, 8, 2, 16, c).transpose(2, 1, 0, 3, 4)
    return jnp.stack([take(a, core, 0), take(a, 1 - core, 0)]).reshape(-1, c)


def panel_of(ordered, p, core):
    c = ordered.shape[-1]
    rows = take(ordered.reshape(2, 8, 4, 16, c), p, 2)
    return jnp.stack([take(rows, core, 0), take(rows, 1 - core, 0)], 1).reshape(-1, c)


def body(cotangent, whitened, panel_rows, diag_inverse):
    device = lax.axis_index("row")
    column = lax.axis_index("col")
    xh, y, core = column // 8, (column // 2) % 4, column % 2
    rows = cotangent.shape[0]
    top = rows - WIDTH
    panels = panel_rows.shape[0]
    owned = 7 - device

    local = jnp.arange(rows, dtype=jnp.int32)
    natural = local // WIDTH * 8 + device
    within = local % WIDTH
    inner = column * 16 + jnp.arange(16, dtype=jnp.int32)
    target = 31 - jnp.arange(panels, dtype=jnp.int32)
    masked = jnp.where((natural[None, :] < target[:, None])[:, None, :], panel_rows, 0.0)
    masked = reorder(masked, core)

    ordered, (masked,) = solve_panels(
        cotangent[top:], panel_rows[: panels - 1, :, top:], device, y, core, [diag_inverse.transpose(0, 2, 1), masked]
    )

    half = 2 * WIDTH
    from_other = lax.ppermute(dot(ordered[half:], whitened, 1, 1), "col", CORE_SWAP)
    kept, from_other = together(dot(ordered[:half], whitened, 1, 1), from_other)
    sums = kept + from_other
    solved = together(ordered, sums)[0]
    residual = cotangent - dot(masked, solved, 0, 0)
    grad = over_eight(sums)
    grad = grad.reshape(panels, 16, rows)
    keep = (natural[None, None, :] < target[:, None, None]) | (
        (natural[None, None, :] == target[:, None, None]) & (inner[None, :, None] >= within[None, None, :])
    )
    grad = jnp.where(keep, -grad, 0.0)

    own = panel_of(solved, jnp.clip(owned, 0, 3), core)
    tail = jnp.where(device >= 4, own, residual[top:])
    residual = lax.dynamic_update_slice_in_dim(residual, tail, top, 0)
    return residual, grad


def solution(mesh):
    return jax.shard_map(
        body,
        mesh=mesh,
        in_specs=(P("row", "col"), P("row", "col"), P(None, None, "row"), P()),
        out_specs=(P("row", "col"), P(None, "col", "row")),
        check_vma=False,
    )
```

```python
import jax
import jax.numpy as jnp
from jax import lax
from jax.experimental import pallas as pl
from jax.experimental.pallas import tpu as pltpu
from jax.sharding import PartitionSpec as P

HIGH = lax.Precision.HIGH
WIDTH = 256


Z_GROUPS = [[2 * z + x for z in range(4)] for x in range(2)]
X_SWAP = [(r, r ^ 1) for r in range(8)]
HALVES = [(7, 3), (6, 2), (5, 1), (4, 0)]
Y_GROUPS = [[(xh * 4 + y) * 2 + core for y in range(4)] for xh in range(2) for core in range(2)]
CORE_SWAP = [(c, c ^ 1) for c in range(16)]
Y_STEPS = [[(c, c // 8 * 8 + (c + 2 * d) % 8) for c in range(16)] for d in (1, 3, 2)]
CORE_GROUPS = [[2 * i + core for i in range(8)] for core in range(2)]


def exchange(pieces, axis, groups=None):
    return lax.all_to_all(pieces, axis, 0, 0, axis_index_groups=groups)


def copies(a, n):
    return jnp.broadcast_to(a[None], (n,) + a.shape)


def together(*arrays):
    return lax.optimization_barrier(arrays)


def take(a, i, axis):
    return lax.dynamic_index_in_dim(a, i, axis, keepdims=False)


def dot(a, b, ca, cb):
    return lax.dot_general(a, b, (((ca,), (cb,)), ((), ())), precision=HIGH, preferred_element_type=jnp.float32)


COUPLED = [(0, 1), (0, 2), (1, 2), (0, 3), (1, 3), (2, 3)]
PART = WIDTH // 8


def couplings_over_row(last, y, core):
    mine = lax.dynamic_slice_in_dim(last, (y * 2 + core) * PART, PART, 1)
    with jax.named_scope("coupling_row"):
        got = exchange(copies(mine.reshape(3 * PART, WIDTH), 8), "row").reshape(8, 3, PART, WIDTH)
    return jnp.concatenate([got[7 - p, q] for q, p in COUPLED], 0)


def couplings_over_y(table):
    with jax.named_scope("coupling_y"):
        return jnp.stack([table] + [lax.ppermute(table, "col", pairs) for pairs in Y_STEPS])


def split(a):
    high = a.astype(jnp.bfloat16)
    return high, (a - high.astype(jnp.float32)).astype(jnp.bfloat16)


def product(a, b):
    def one(s, t):
        return jnp.dot(s, t, preferred_element_type=jnp.float32)

    return one(a[0], b[0]) + (one(a[0], b[1]) + one(a[1], b[0]))


def solve_kernel(
    place, over_z, peer, both, same, swapped, diagonal, ordered, raw, coupling, left_high, left_low, high, low
):
    x, y_index, core = place[0], place[1], place[2]

    @pl.when(pl.program_id(0) == 0)
    def _():
        for r, back in enumerate((0, 1, 3, 2)):
            from_y = lax.rem(y_index + (4 - back), 4)
            for part, c in ((same, core), (swapped, 1 - core)):
                start = pl.multiple_of((from_y * 2 + c) * PART, PART)
                for i in range(6):
                    coupling[i, pl.ds(start, PART)] = part[r, PART * i : PART * (i + 1)]
        for i, (q, p) in enumerate(COUPLED):
            at = slice(WIDTH * q, WIDTH * (q + 1))
            left_high[p, :, at], left_low[p, :, at] = split(coupling[i].T)
        for p in range(4):
            at = slice(WIDTH * p, WIDTH * (p + 1))
            left_high[p, :, at], left_low[p, :, at] = split(diagonal[p])

    for pair, z in ((0, 3), (1, 2)):
        mine = [over_z[z], both[z, 0], over_z[z - 2], both[z - 2, 0]]
        other = [peer[z], both[z, 1], peer[z - 2], both[z - 2, 1]]
        for i in range(4):
            for panel, part in ((1 - x, mine[i]), (x, other[i])):
                raw[pl.ds(pl.multiple_of((2 * pair + panel) * WIDTH + 64 * i, 64), 64)] = part
    for p in range(4):
        done, at = slice(0, WIDTH * p), slice(WIDTH * p, WIDTH * (p + 1))
        acc = raw[at]
        if p:
            acc = acc - product((left_high[p, :, done], left_low[p, :, done]), (high[done], low[done]))
        y = product((left_high[p, :, at], left_low[p, :, at]), split(acc))
        for i in range(8):
            for c in range(2):
                to, of = lax.bitwise_xor(core, c) * 512 + i * 64 + p * 16, 16 * (i * 2 + c)
                ordered[pl.ds(pl.multiple_of(to, 16), 16)] = y[of : of + 16]
        if p < 3:
            high[at], low[at] = split(y)


def solve(place, over_z, peer, both, same, swapped, diagonal):
    rows = over_z.shape[-1]
    tile = 1024
    whole = pl.BlockSpec((4, 6 * PART, WIDTH), lambda j: (0, 0, 0), pipeline_mode=pl.Buffered(1))
    return pl.pallas_call(
        solve_kernel,
        out_shape=jax.ShapeDtypeStruct((4 * WIDTH, rows), jnp.float32),
        grid=(rows // tile,),
        in_specs=[
            pl.BlockSpec(memory_space=pltpu.SMEM),
            pl.BlockSpec((4, 64, tile), lambda j: (0, 0, j)),
            pl.BlockSpec((4, 64, tile), lambda j: (0, 0, j)),
            pl.BlockSpec((4, 2, 64, tile), lambda j: (0, 0, 0, j)),
            whole,
            whole,
            pl.BlockSpec((4, WIDTH, WIDTH), lambda j: (0, 0, 0), pipeline_mode=pl.Buffered(1)),
        ],
        out_specs=pl.BlockSpec((4 * WIDTH, tile), lambda j: (0, j)),
        scratch_shapes=[
            pltpu.VMEM((4 * WIDTH, tile), jnp.float32),
            pltpu.VMEM((6, WIDTH, WIDTH), jnp.float32),
            pltpu.VMEM((4, WIDTH, 4 * WIDTH), jnp.bfloat16),
            pltpu.VMEM((4, WIDTH, 4 * WIDTH), jnp.bfloat16),
            pltpu.VMEM((3 * WIDTH, tile), jnp.bfloat16),
            pltpu.VMEM((3 * WIDTH, tile), jnp.bfloat16),
        ],
        compiler_params=pltpu.CompilerParams(vmem_limit_bytes=40 * 1024 * 1024),
        cost_estimate=pl.CostEstimate(flops=6 * 10 * WIDTH * WIDTH * rows, bytes_accessed=11 * 2**20, transcendentals=0),
    )(place, over_z, peer, both, same, swapped, diagonal)


def solve_panels(block, last, device, y, core, early):
    half = block.shape[0] // 2
    table = couplings_over_row(last, y, core)
    with jax.named_scope("halves"):
        sent = lax.ppermute(block[half:], "row", HALVES)
    shard = jnp.where(device >= 4, block[:half], sent)
    a, b = shard[: half // 2], shard[half // 2 :]
    with jax.named_scope("first"):
        a, b, table, *early = together(a, b, table, *early)
        over_z = exchange(copies(a, 4), "row", Z_GROUPS)
        over_x = lax.ppermute(b, "row", X_SWAP)
        over_z, second, same = together(over_z, jnp.concatenate([b, over_x], 0), couplings_over_y(table))
    with jax.named_scope("second"):
        both = exchange(copies(second, 4), "row", Z_GROUPS)
        peer = lax.ppermute(over_z, "row", X_SWAP)
        swapped = lax.ppermute(same, "col", CORE_SWAP)
    both = both.reshape(4, 2, half // 2, -1)
    place = jnp.stack([device % 2, y, core])
    return solve(place, over_z, peer, both, same, swapped, early[0]), early[1:]


def over_eight(a):
    return exchange(a.reshape(8, -1, a.shape[-1]), "col", CORE_GROUPS).sum(0)


def reorder(a, core):
    c = a.shape[-1]
    a = a.reshape(4, 8, 2, 16, c).transpose(2, 1, 0, 3, 4)
    return jnp.stack([take(a, core, 0), take(a, 1 - core, 0)]).reshape(-1, c)


def panel_of(ordered, p, core):
    c = ordered.shape[-1]
    rows = take(ordered.reshape(2, 8, 4, 16, c), p, 2)
    return jnp.stack([take(rows, core, 0), take(rows, 1 - core, 0)], 1).reshape(-1, c)


def body(cotangent, whitened, panel_rows, diag_inverse):
    device = lax.axis_index("row")
    column = lax.axis_index("col")
    xh, y, core = column // 8, (column // 2) % 4, column % 2
    rows = cotangent.shape[0]
    top = rows - WIDTH
    panels = panel_rows.shape[0]
    owned = 7 - device

    local = jnp.arange(rows, dtype=jnp.int32)
    natural = local // WIDTH * 8 + device
    within = local % WIDTH
    inner = column * 16 + jnp.arange(16, dtype=jnp.int32)
    target = 31 - jnp.arange(panels, dtype=jnp.int32)
    masked = jnp.where((natural[None, :] < target[:, None])[:, None, :], panel_rows, 0.0)
    masked = reorder(masked, core)

    ordered, (masked,) = solve_panels(
        cotangent[top:], panel_rows[: panels - 1, :, top:], device, y, core, [diag_inverse.transpose(0, 2, 1), masked]
    )

    half = 2 * WIDTH
    from_other = lax.ppermute(dot(ordered[half:], whitened, 1, 1), "col", CORE_SWAP)
    kept, from_other = together(dot(ordered[:half], whitened, 1, 1), from_other)
    sums = kept + from_other
    solved = together(ordered, sums)[0]
    residual = cotangent - dot(masked, solved, 0, 0)
    grad = over_eight(sums)
    grad = grad.reshape(panels, 16, rows)
    keep = (natural[None, None, :] < target[:, None, None]) | (
        (natural[None, None, :] == target[:, None, None]) & (inner[None, :, None] >= within[None, None, :])
    )
    grad = jnp.where(keep, -grad, 0.0)

    own = panel_of(solved, jnp.clip(owned, 0, 3), core)
    tail = jnp.where(device >= 4, own, residual[top:])
    residual = lax.dynamic_update_slice_in_dim(residual, tail, top, 0)
    return residual, grad


def solution(mesh):
    return jax.shard_map(
        body,
        mesh=mesh,
        in_specs=(P("row", "col"), P("row", "col"), P(None, None, "row"), P()),
        out_specs=(P("row", "col"), P(None, "col", "row")),
        check_vma=False,
    )
```
